128 devices in a mesh: grp: 8 (over z_lo, x), own: 16 (over y, z_hi, core).
Axes of the slice: x: 4, y: 4, z: 4 (z_hi: 2, z_lo: 2; z = z_hi * 2 + z_lo), core: 2. Of those that a mesh axis runs over, the one named last changes fastest.
Arguments:
- hidden_in: bfloat16 [16, 2048, 1024], P('own', 'grp'), may hold values from -6 to 6
- cotangent: bfloat16 [16, 2048, 1024], P('own', 'grp'), may hold values from -6 to 6
- segment_ids: int32 [16, 2048], P('own'), may hold values from 0 to 12, as said below
- live_slots: int32 [16, 2048], P('own'), may hold values from 0 to 1, as said below
- w_qkv: bfloat16 [1024, 3072], P('grp'), may hold values from -0.1875 to 0.1875
- w_out: bfloat16 [1024, 1024], P('grp'), may hold values from -0.75 to 0.75
- w_up: bfloat16 [1024, 4096], P('grp'), may hold values from -0.1875 to 0.1875
- w_down: bfloat16 [4096, 1024], P('grp'), may hold values from -0.09375 to 0.09375
- w_vec: bfloat16 [1024, 13], P('grp'), as said below
- master_qkv: float32 [1024, 3072], P('grp'), may hold values from -0.1875 to 0.1875
- master_out: float32 [1024, 1024], P('grp'), may hold values from -0.75 to 0.75
- master_up: float32 [1024, 4096], P('grp'), may hold values from -0.1875 to 0.1875
- master_down: float32 [4096, 1024], P('grp'), may hold values from -0.09375 to 0.09375
- master_vec: float32 [1024, 13], P('grp'), as said below
- first_qkv: float32 [1024, 3072], P('grp'), may hold values from -2048 to 2048
- first_out: float32 [1024, 1024], P('grp'), may hold values from -320 to 320
- first_up: float32 [1024, 4096], P('grp'), may hold values from -256 to 256
- first_down: float32 [4096, 1024], P('grp'), may hold values from -640 to 640
- first_vec: float32 [1024, 13], P('grp'), may hold values from -1024 to 1024
- second_qkv: float32 [1024, 3072], P('grp'), may hold values from 65536 to 1048576
- second_out: float32 [1024, 1024], P('grp'), may hold values from 1474.56 to 23592.96
- second_up: float32 [1024, 4096], P('grp'), may hold values from 983.04 to 16384
- second_down: float32 [4096, 1024], P('grp'), may hold values from 5898.24 to 94371.84
- second_vec: float32 [1024, 13], P('grp'), may hold values from 16384 to 262144
Outputs:
- layer_out: bfloat16 [16, 2048, 1024], P('own', 'grp')
- input_grad: float32 [16, 2048, 1024], P('own', 'grp')
- new_master_qkv: float32 [1024, 3072], P('grp')
- new_master_out: float32 [1024, 1024], P('grp')
- new_master_up: float32 [1024, 4096], P('grp')
- new_master_down: float32 [4096, 1024], P('grp')
- new_master_vec: float32 [1024, 13], P('grp')
- new_first_qkv: float32 [1024, 3072], P('grp')
- new_first_out: float32 [1024, 1024], P('grp')
- new_first_up: float32 [1024, 4096], P('grp')
- new_first_down: float32 [4096, 1024], P('grp')
- new_first_vec: float32 [1024, 13], P('grp')
- new_second_qkv: float32 [1024, 3072], P('grp')
- new_second_out: float32 [1024, 1024], P('grp')
- new_second_up: float32 [1024, 4096], P('grp')
- new_second_down: float32 [4096, 1024], P('grp')
- new_second_vec: float32 [1024, 13], P('grp')
- copy_qkv: bfloat16 [1024, 3072], P('grp')
- copy_out: bfloat16 [1024, 1024], P('grp')
- copy_up: bfloat16 [1024, 4096], P('grp')
- copy_down: bfloat16 [4096, 1024], P('grp')
- copy_vec: bfloat16 [1024, 13], P('grp')
The draws below stay inside these ranges and needn't reach their ends.
Inputs may be any that keep to these rules, and one draw needn't show every extreme that they name: `segment_ids`: each row holds one tree in depth-first order: trunk (segment 0), then for branch b = 1 to 4 the branch (segment b) followed by its two leaves (segments 2 b + 3 and 2 b + 4); a branch has 64 to 128 slots, a leaf 64 // 2 to 64; the trunk fills the row but for fewer than 32 slots after the last leaf, which carry segment 12. `live_slots`: 1 exactly on the slots of the tree, 0 on the slots after it. `w_vec`: columns 0 and 2 lie in 0.6 to 1.4, the others in -0.2 to 0.2. `master_vec`: columns 0 and 2 lie in 0.6 to 1.4, the others in -0.2 to 0.2.
All inputs are finite; a program needn't handle non-finite values.
Results may differ from the reference program's by a relative error of at most 0.003.
The reference program's roundings to bfloat16 on the way count: a program that leaves them out, or rounds other values in their place, can miss the bound.
Values may be sent and summed in bfloat16 or wider, within the bound.
No kernel may reach another device: no remote copies, remote signals or barrier semaphores. Data moves between devices by JAX's collectives and lax.ppermute only.
A program may use at most 320 MiB of HBM per device.

```python
import math
import jax
import jax.numpy as jnp
from jax import lax

D = 1024
HEADS = 16
HD = 64
FF = 4096
ROT = 16
BRANCH = 128
LEAF = 64
SEQ = 2048
ROWS_DEV = 1
ROWS = 16
NVEC = 13
STEP = 5
N_OWN = 16


def tree_layout(key):
    order_table = jnp.array([0, 1, 5, 6, 2, 7, 8, 3, 9, 10, 4, 11, 12], jnp.int32)
    capacity = jnp.array([BRANCH, LEAF, LEAF] * 4, jnp.int32)
    sized = jax.random.randint(key, (ROWS, 12), capacity // 2, capacity + 1)
    padding = jax.random.randint(jax.random.fold_in(key, 5), (ROWS, 1), 0, LEAF // 2)
    trunk_len = SEQ - padding - jnp.sum(sized, axis=1, keepdims=True)
    lengths = jnp.concatenate([trunk_len, sized], axis=1)
    ends = jnp.cumsum(lengths, axis=1)
    slots = jnp.arange(SEQ, dtype=jnp.int32)
    position = jnp.sum((slots[None, :, None] >= ends[:, None, :]).astype(jnp.int32), axis=2)
    position = jnp.minimum(position, 12)
    picker = (position[..., None] == jnp.arange(13, dtype=jnp.int32)).astype(jnp.int32)
    segment = jnp.sum(picker * order_table, axis=-1)
    live_row = (slots[None, :] < ends[:, -1:]).astype(jnp.int32)
    return (segment, live_row)


def draw_segment_ids(key, part):
    shared = tree_layout(key)
    return shared[0]


def draw_live_slots(key, part):
    shared = tree_layout(key)
    return shared[1]


def vector_law(key):
    base = jax.random.uniform(key, (D, NVEC), jnp.float32, -0.2, 0.2)
    column = jnp.arange(NVEC)[None, :]
    gains = (column == 0) | (column == 2)
    return jnp.where(gains, 1.0 + 2.0 * base, base)


def draw_w_vec(key, part):
    key = jax.random.fold_in(key, 21)
    return vector_law(key).astype(jnp.bfloat16)


def draw_master_vec(key, part):
    key = jax.random.fold_in(key, 22)
    return vector_law(key)


def level_of(own_key, extent, pieces, least, top_value):
    gain = 1.0
    for dim, parts in pieces:
        heights = jax.random.uniform(jax.random.fold_in(jax.random.fold_in(own_key, 6), dim), (parts,), jnp.float32, least / len(pieces), top_value / len(pieces))
        gain = gain * jnp.repeat(jnp.exp(heights), extent[dim] // parts).reshape((-1,) + (1,) * (len(extent) - 1 - dim))
    return gain


def scatter_about(own_key, dims, scale, limit, shards=(), held_as=jnp.bfloat16):
    level = level_of(own_key, dims, shards, -0.22, 0.18) if shards else 1.0
    values = jax.random.normal(own_key, dims, jnp.float32) * scale * level
    return jnp.minimum(jnp.maximum(values, -limit), limit).astype(held_as)


def setup_inputs(seed: int = 0) -> dict:
    keys = jax.random.split(jax.random.key(seed), 25)
    return {
        "hidden_in": scatter_about(keys[0], (ROWS, SEQ, D), 1.0, 6.0, ((0, 16), (1, 8))),
        "cotangent": scatter_about(keys[1], (ROWS, SEQ, D), 1.0, 6.0, ((0, 16), (1, 8))),
        "segment_ids": draw_segment_ids(jax.random.fold_in(keys[24], 71), 0),
        "live_slots": draw_live_slots(jax.random.fold_in(keys[24], 71), 0),
        "w_qkv": scatter_about(keys[4], (D, 3 * D), D ** -0.5, 0.1875, ((0, 8),)),
        "w_out": scatter_about(keys[5], (D, D), (D // 16) ** -0.5, 0.75, ((0, 8),)),
        "w_up": scatter_about(keys[6], (D, FF), D ** -0.5, 0.1875, ((0, 8),)),
        "w_down": scatter_about(keys[7], (FF, D), FF ** -0.5, 0.09375, ((0, 8),)),
        "w_vec": draw_w_vec(jax.random.fold_in(keys[24], 71), 0),
        "master_qkv": scatter_about(keys[9], (D, 3 * D), D ** -0.5, 0.1875, ((0, 8),), jnp.float32),
        "master_out": scatter_about(keys[10], (D, D), (D // 16) ** -0.5, 0.75, ((0, 8),), jnp.float32),
        "master_up": scatter_about(keys[11], (D, FF), D ** -0.5, 0.1875, ((0, 8),), jnp.float32),
        "master_down": scatter_about(keys[12], (FF, D), FF ** -0.5, 0.09375, ((0, 8),), jnp.float32),
        "master_vec": draw_master_vec(jax.random.fold_in(keys[24], 71), 0),
        "first_qkv": scatter_about(keys[14], (D, 3 * D), (2.0 * (ROWS_DEV * N_OWN * SEQ) ** 0.5), 2048.0, ((0, 8),), jnp.float32),
        "first_out": scatter_about(keys[15], (D, D), (0.3 * (ROWS_DEV * N_OWN * SEQ) ** 0.5), 320.0, ((0, 8),), jnp.float32),
        "first_up": scatter_about(keys[16], (D, FF), (0.25 * (ROWS_DEV * N_OWN * SEQ) ** 0.5), 256.0, ((0, 8),), jnp.float32),
        "first_down": scatter_about(keys[17], (FF, D), (0.6 * (ROWS_DEV * N_OWN * SEQ) ** 0.5), 640.0, ((0, 8),), jnp.float32),
        "first_vec": scatter_about(keys[18], (D, NVEC), (1.0 * (ROWS_DEV * N_OWN * SEQ) ** 0.5), 1024.0, ((0, 8),), jnp.float32),
        "second_qkv": jnp.clip(jnp.exp(math.log(1048576) - 2.7725887 * jax.random.uniform(keys[19], (D, 3 * D), jnp.float32) ** level_of(keys[19], (D, 3 * D), ((0, 8),), -0.2, 0.2)), 65536.0, 1048576),
        "second_out": jnp.clip(jnp.exp(math.log(23592.96) - 2.7725887 * jax.random.uniform(keys[20], (D, D), jnp.float32) ** level_of(keys[20], (D, D), ((0, 8),), -0.2, 0.2)), 1474.56, 23592.96),
        "second_up": jnp.clip(jnp.exp(math.log(16384.0) - 2.8134107 * jax.random.uniform(keys[21], (D, FF), jnp.float32) ** level_of(keys[21], (D, FF), ((0, 8),), -0.2, 0.2)), 983.04, 16384.0),
        "second_down": jnp.clip(jnp.exp(math.log(94371.84) - 2.7725887 * jax.random.uniform(keys[22], (FF, D), jnp.float32) ** level_of(keys[22], (FF, D), ((0, 8),), -0.2, 0.2)), 5898.24, 94371.84),
        "second_vec": jnp.clip(jnp.exp(math.log(262144.0) - 2.7725887 * jax.random.uniform(keys[23], (D, NVEC), jnp.float32) ** level_of(keys[23], (D, NVEC), ((0, 8),), -0.2, 0.2)), 16384.0, 262144.0),
    }


@jax.custom_vjp
def low(v):
    return lax.optimization_barrier(v.astype(jnp.bfloat16)).astype(jnp.float32)

@jax.custom_vjp
def low_back(v):
    return v

def low_keep(v):
    return (low(v), None)

def low_pass(kept, grad):
    return (grad,)

def back_keep(v):
    return (v, None)

def back_low(kept, grad):
    return (low(grad),)
low.defvjp(low_keep, low_pass)
low_back.defvjp(back_keep, back_low)
norm_eps = 1e-05
adam_beta = 0.5
adam_eps = 1e-08
weight_decay = 0.01
learn_rates = (0.02, 0.1, 0.02, 0.01, 0.2)
highest = lax.Precision.HIGHEST

def layer_norm(inputs, gain_vec, shift_vec):
    center = inputs - lax.optimization_barrier(jnp.mean(inputs, axis=-1, keepdims=True))
    spread = lax.optimization_barrier(jnp.mean(center * center, axis=-1, keepdims=True))
    return center * lax.rsqrt(spread + norm_eps) * gain_vec + shift_vec

def rotary(tensor, cos_table, sin_table):
    half_dim = ROT // 2
    front_half = tensor[..., :half_dim]
    back_half = tensor[..., half_dim:ROT]
    cos_part = cos_table[:, None, :]
    sin_part = sin_table[:, None, :]
    return jnp.concatenate([front_half * cos_part - back_half * sin_part, back_half * cos_part + front_half * sin_part, tensor[..., ROT:]], axis=-1)

def branch_of(segment):
    return jnp.where(segment >= 5, 1 + (segment - 5) // 2, segment)

def path_mask(query_seg, key_seg, query_pos, key_pos, key_live):
    same_seg = key_seg[None, :] == query_seg[:, None]
    trunk_key = key_seg[None, :] == 0
    parent_key = (query_seg[:, None] >= 5) & (key_seg[None, :] == branch_of(query_seg)[:, None])
    causal = key_pos[None, :] <= query_pos[:, None]
    return (same_seg | trunk_key | parent_key) & causal & (key_live[None, :] == 1)

def row_forward(inputs, wqkv, wout, wup, wdown, vectors, segment, live_row):
    length = inputs.shape[0]
    bias_up = vectors[:, 9:].T.reshape(FF)
    bias_qkv = jnp.concatenate([vectors[:, 4], vectors[:, 5], vectors[:, 6]])
    norm_one = low(layer_norm(inputs, vectors[:, 0], vectors[:, 1]))
    projected = low_back(jnp.dot(norm_one, wqkv, precision=highest) + bias_qkv)
    positions = jnp.arange(length).astype(jnp.float32)
    inv_freq = 10000.0 ** (-jnp.arange(0, ROT, 2).astype(jnp.float32) / ROT)
    angles = positions[:, None] * inv_freq[None, :]
    cos_table = jnp.cos(angles)
    sin_table = jnp.sin(angles)
    queries = low(rotary(projected[:, :D].reshape(length, HEADS, HD), cos_table, sin_table))
    key_all = low(rotary(projected[:, D:2 * D].reshape(length, HEADS, HD), cos_table, sin_table))
    values = low(projected[:, 2 * D:].reshape(length, HEADS, HD))
    slot_index = jnp.arange(length).astype(jnp.int32)
    query_block = 512 if length % 512 == 0 else length
    scale = 1.0 / math.sqrt(HD)

    def attend(block_start):
        query_part = lax.dynamic_slice_in_dim(queries, block_start, query_block, 0)
        seg_part = lax.dynamic_slice_in_dim(segment, block_start, query_block, 0)
        pos_part = lax.dynamic_slice_in_dim(slot_index, block_start, query_block, 0)
        scores = low_back(jnp.einsum('qhd,khd->hqk', query_part, key_all, precision=highest) * scale)
        allowed = path_mask(seg_part, segment, pos_part, slot_index, live_row)
        scores = jnp.where(allowed[None], scores, -1e+30)
        row_max = lax.optimization_barrier(jnp.max(scores, axis=-1, keepdims=True))
        exp_scores = jnp.exp(scores - row_max)
        attn_probs = low(exp_scores / lax.optimization_barrier(jnp.sum(exp_scores, axis=-1, keepdims=True)))
        return jnp.einsum('hqk,khd->qhd', attn_probs, values, precision=highest)
    starts = jnp.arange(0, length, query_block).astype(jnp.int32)
    attn = lax.map(jax.checkpoint(attend), starts).reshape(length, D)
    attn = low(low_back(attn))
    out_attn = jnp.dot(attn, wout, precision=highest) + vectors[:, 7]
    norm_two = low(layer_norm(inputs, vectors[:, 2], vectors[:, 3]))
    pre_act = low_back(jnp.dot(norm_two, wup, precision=highest) + bias_up)
    act_low = low(jax.nn.gelu(pre_act, approximate=False))
    out_mlp = jnp.dot(act_low, wdown, precision=highest) + vectors[:, 8]
    return inputs + out_attn + out_mlp

def adamw_update(master, first_mom, second_mom, gradient, learn_rate):
    first_new = adam_beta * first_mom + (1.0 - adam_beta) * gradient
    second_new = adam_beta * second_mom + (1.0 - adam_beta) * gradient * gradient
    correction = 1.0 - adam_beta ** STEP
    adam_step = first_new / correction / (jnp.sqrt(second_new / correction) + adam_eps)
    master_new = master - learn_rate * (adam_step + weight_decay * master)
    return (master_new, first_new, second_new)

def reference(hidden_in, cotangent, segment_ids, live_slots, w_qkv, w_out, w_up, w_down, w_vec, master_qkv, master_out, master_up, master_down, master_vec, first_qkv, first_out, first_up, first_down, first_vec, second_qkv, second_out, second_up, second_down, second_vec):
    weights = tuple((item.astype(jnp.float32) for item in (w_qkv, w_out, w_up, w_down, w_vec)))

    def one_row(totals, row_data):
        inputs, back_row, segment, live_row = row_data

        def forward(row_inputs, wqkv, wout, wup, wdown, vectors):
            return row_forward(row_inputs, wqkv, wout, wup, wdown, vectors, segment, live_row)
        output, pullback = jax.vjp(forward, inputs.astype(jnp.float32), *weights)
        gradients = pullback(back_row.astype(jnp.float32))
        totals = tuple((total + gradient for total, gradient in zip(totals, gradients[1:])))
        return (totals, (output.astype(jnp.bfloat16), gradients[0]))
    zeros_start = tuple((jnp.zeros(item.shape, jnp.float32) for item in weights))
    sums, outputs = lax.scan(one_row, zeros_start, (hidden_in, cotangent, segment_ids, live_slots))
    layer_out, input_grad = outputs
    masters = (master_qkv, master_out, master_up, master_down, master_vec)
    firsts = (first_qkv, first_out, first_up, first_down, first_vec)
    seconds = (second_qkv, second_out, second_up, second_down, second_vec)
    news = [adamw_update(masters[which], firsts[which], seconds[which], sums[which], learn_rates[which]) for which in range(5)]
    return (layer_out, input_grad, news[0][0], news[1][0], news[2][0], news[3][0], news[4][0], news[0][1], news[1][1], news[2][1], news[3][1], news[4][1], news[0][2], news[1][2], news[2][2], news[3][2], news[4][2], news[0][0].astype(jnp.bfloat16), news[1][0].astype(jnp.bfloat16), news[2][0].astype(jnp.bfloat16), news[3][0].astype(jnp.bfloat16), news[4][0].astype(jnp.bfloat16))
```

```python
import math

import jax
import jax.numpy as jnp
from jax import lax
from jax.experimental import pallas as pl
from jax.experimental.pallas import tpu as pltpu
from jax.sharding import PartitionSpec as P

HEADS = 16
HD = 64
ROT = 16
STEP = 5
BLK = 256
QBLK = 512
KBLK = 512

norm_eps = 1e-05
adam_beta = 0.5
adam_eps = 1e-08
weight_decay = 0.01
learn_rates = (0.02, 0.1, 0.02, 0.01, 0.2)
scale = 1.0 / math.sqrt(HD)
log2e = 1.4426950408889634
soft_mul = scale * log2e
f32 = jnp.float32
low = jnp.bfloat16

erfc_terms = (
    0.17087277,
    -0.82215223,
    1.48851587,
    -1.13520398,
    0.27886807,
    -0.18628806,
    0.09678418,
    0.37409196,
    1.00002368,
    -1.26551223,
)


def params(limit=56):
    return pltpu.CompilerParams(
        dimension_semantics=("arbitrary",), vmem_limit_bytes=limit * 1024 * 1024
    )


def cost(micros):
    return pl.CostEstimate(
        flops=int(micros * 1e8), bytes_accessed=int(micros * 3e5), transcendentals=0
    )


def mm(left, right):
    return lax.dot_general(left, right, (((1,), (0,)), ((), ())), preferred_element_type=f32)


def mm_nt(left, right):
    return lax.dot_general(left, right, (((1,), (1,)), ((), ())), preferred_element_type=f32)


def mm_tn(left, right):
    return lax.dot_general(left, right, (((0,), (0,)), ((), ())), preferred_element_type=f32)


def whole(shape):
    return pl.BlockSpec(shape, lambda i, *_: (0,) * len(shape))


unread = pl.BlockSpec(memory_space=pl.ANY)


def normalize(inputs):
    center = inputs - jnp.mean(inputs, axis=-1, keepdims=True)
    inverse = lax.rsqrt(jnp.mean(center * center, axis=-1, keepdims=True) + norm_eps)
    return (center * inverse, inverse)


def norm_back(grad_norm, normed, inverse):
    mean_one = jnp.mean(grad_norm, axis=-1, keepdims=True)
    mean_two = jnp.mean(grad_norm * normed, axis=-1, keepdims=True)
    return inverse * (grad_norm - mean_one - normed * mean_two)


def turn(tensor, cos_full, sin_front, sin_back, direction):
    ahead = pltpu.roll(tensor, 120, 1)
    behind = pltpu.roll(tensor, 8, 1)
    return tensor * cos_full + direction * (ahead * sin_front + behind * sin_back)


def gelu_parts(pre):
    size = jnp.abs(pre) * math.sqrt(0.5)
    inv = 1.0 / (1.0 + 0.5 * size)
    poly = jnp.full_like(pre, erfc_terms[0])
    for term in erfc_terms[1:]:
        poly = poly * inv + term
    square = size * size
    tail = 0.5 * inv * jnp.exp(poly - square)
    cdf = jnp.where(pre >= 0.0, 1.0 - tail, tail)
    bell = jnp.exp(-square) * (1.0 / math.sqrt(2.0 * math.pi))
    return pre * cdf, cdf + pre * bell


def enter_kernel(
    x_ref, w_ref, rows_ref, bq_ref, bu_ref, cos_ref, sf_ref, sb_ref,
    *rest
):
    q_ref, k_ref, v_ref, kt_ref, vt_ref, n1_ref, n2_ref, act_ref, slope_ref, cols_ref = rest[-10:]

    @pl.when(pl.program_id(0) == 0)
    def _():
        for g in range(w_ref.shape[1]):
            for u in range(w_ref.shape[0]):
                top = g * 128 + u * 16
                cols_ref[top : top + 16, :] = w_ref[u, g]

    normed, _ = normalize(x_ref[...].astype(f32))
    n1 = (normed * rows_ref[0:1] + rows_ref[1:2]).astype(low)
    n2 = (normed * rows_ref[2:3] + rows_ref[3:4]).astype(low)
    n1_ref[...] = n1
    n2_ref[...] = n2
    part = q_ref.shape[1]
    ff = act_ref.shape[1]
    proj = mm(n1, cols_ref[:, : 3 * part]) + bq_ref[...]
    tables = (cos_ref[...], sf_ref[...], sb_ref[...])
    q_ref[...] = turn(proj[:, :part], *tables, 1.0).astype(low)
    key = turn(proj[:, part : 2 * part], *tables, 1.0)
    value = proj[:, 2 * part :]
    k_ref[...] = key.astype(low)
    v_ref[...] = value.astype(low)
    kt_ref[0] = key.T.astype(low)
    vt_ref[0] = value.T.astype(low)
    act, slope = gelu_parts(mm(n2, cols_ref[:, 3 * part : 3 * part + ff]) + bu_ref[...])
    act_ref[...] = act.astype(low)
    slope_ref[...] = slope


def enter(x_row, wide, rows, bias_qkv, bias_up, tables, after):
    seq, width = x_row.shape
    part = bias_qkv.shape[1] // 3
    ff = bias_up.shape[1]
    cols = (width, wide.shape[3])
    steps = seq // BLK
    blk = lambda cols: pl.BlockSpec((BLK, cols), lambda i: (i, 0))
    flip = pl.BlockSpec((1, part, BLK), lambda i: (i, 0, 0))
    shape = jax.ShapeDtypeStruct
    return pl.pallas_call(
        enter_kernel,
        grid=(steps,),
        in_specs=[
            blk(width), whole(wide.shape), whole(rows.shape),
            whole(bias_qkv.shape), whole(bias_up.shape), blk(part), blk(part), blk(part),
        ]
        + [unread] * len(after),
        out_specs=[blk(part)] * 3 + [flip] * 2 + [blk(width)] * 2 + [blk(ff)] * 2 + [whole(cols)],
        out_shape=[shape((seq, part), low)] * 3
        + [shape((steps, part, BLK), low)] * 2
        + [shape((seq, width), low)] * 2
        + [shape((seq, ff), low), shape((seq, ff), f32), shape(cols, low)],
        compiler_params=params(),
        cost_estimate=cost(17),
        name="enter",
    )(x_row, wide, rows, bias_qkv, bias_up, *tables, *after)


def split_heads(block):
    lane = lax.broadcasted_iota(jnp.int32, block.shape, 1)
    wide = block.astype(f32)
    return (
        jnp.where(lane < HD, wide, 0.0).astype(low),
        jnp.where(lane >= HD, wide, 0.0).astype(low),
    )


def allowed_keys(kseg_ref, qinfo_ref, j, i):
    key_part = kseg_ref[pl.ds(j * KBLK, KBLK), :]
    key_seg = jnp.concatenate([key_part] * (QBLK // 128), axis=1)
    key_pos = lax.broadcasted_iota(jnp.int32, (KBLK, QBLK), 0) + j * KBLK
    query_pos = lax.broadcasted_iota(jnp.int32, (KBLK, QBLK), 1) + i * QBLK
    same = (key_seg == qinfo_ref[0, 0:1, :]) | (key_seg == qinfo_ref[0, 1:2, :]) | (key_seg == 0)
    return same & (key_pos <= query_pos)


def fold_rows(tile, how):
    return how(tile.reshape(tile.shape[0] // 8, 8, tile.shape[1]), axis=0)


def each_block(i, trunk, count, run):
    def step(j, carry):
        end = (j + 1) * KBLK
        open_block = (end <= i * QBLK) & (end <= trunk)

        @pl.when(open_block)
        def _():
            run(j, False)

        @pl.when(jnp.logical_not(open_block))
        def _():
            run(j, True)

        return carry

    lax.fori_loop(0, count, step, 0)


def forward_kernel(
    trunk_ref, q_ref, k_ref, vt_ref, qinfo_ref, kseg_ref,
    attn_ref, lse_ref, s_scr, m_scr, l_scr, o_scr,
):
    i = pl.program_id(0)
    heads = split_heads(q_ref[...])
    count = i * QBLK // KBLK + 1
    m_scr[...] = jnp.full(m_scr.shape, -3e38, f32)

    def scores(j, masked):
        keys = k_ref[pl.ds(j * KBLK, KBLK), :]
        allowed = allowed_keys(kseg_ref, qinfo_ref, j, i) if masked else None
        for h in range(2):
            tile = mm_nt(keys, heads[h])
            if masked:
                tile = jnp.where(allowed, tile, -1e30)
            s_scr[h, j] = tile
            m_scr[h] = jnp.maximum(m_scr[h], fold_rows(tile, jnp.max))

    each_block(i, trunk_ref[0], count, scores)
    tops = [jnp.max(m_scr[h], axis=0, keepdims=True) * soft_mul for h in range(2)]
    l_scr[...] = jnp.zeros(l_scr.shape, f32)

    def exps(j, carry):
        for h in range(2):
            tile = jnp.exp2(s_scr[h, j] * soft_mul - tops[h])
            s_scr[h, j] = tile
            l_scr[h] += fold_rows(tile, jnp.sum)
        return carry

    lax.fori_loop(0, count, exps, 0)
    sums = [jnp.sum(l_scr[h], axis=0, keepdims=True) for h in range(2)]
    invs = [1.0 / total for total in sums]
    for h in range(2):
        lse_ref[0, h : h + 1, :] = tops[h] + jnp.log(sums[h]) * log2e
    o_scr[...] = jnp.zeros(o_scr.shape, f32)

    def weigh(j, carry):
        for h in range(2):
            probs = (s_scr[h, j] * invs[h]).astype(low)
            rows = slice(h * HD, (h + 1) * HD)
            o_scr[rows, :] += mm(vt_ref[2 * j, rows, :], probs[:BLK]) + mm(
                vt_ref[2 * j + 1, rows, :], probs[BLK:]
            )
        return carry

    lax.fori_loop(0, count, weigh, 0)
    attn_ref[...] = o_scr[...].T.astype(low)


def attend_forward(trunk, q, k, vt, qinfo, kseg):
    seq, part = q.shape
    steps = seq // QBLK
    blk = pl.BlockSpec((QBLK, part), lambda i, t: (i, 0))
    info = pl.BlockSpec((1, 8, QBLK), lambda i, t: (i, 0, 0))
    shape = jax.ShapeDtypeStruct
    return pl.pallas_call(
        forward_kernel,
        grid_spec=pltpu.PrefetchScalarGridSpec(
            num_scalar_prefetch=1,
            grid=(steps,),
            in_specs=[blk, whole(k.shape), whole(vt.shape), info, whole(kseg.shape)],
            out_specs=[blk, info],
            scratch_shapes=[
                pltpu.VMEM((2, seq // KBLK, KBLK, QBLK), f32),
                pltpu.VMEM((2, 8, QBLK), f32),
                pltpu.VMEM((2, 8, QBLK), f32),
                pltpu.VMEM((part, QBLK), f32),
            ],
        ),
        out_shape=[shape((seq, part), low), shape((steps, 8, QBLK), f32)],
        compiler_params=params(),
        cost_estimate=cost(19),
        name="attend_forward",
    )(trunk, q, k, vt, qinfo, kseg)


def merge_kernel(place_ref, attn_ref, act_ref, wo_ref, wd_ref, out_ref):
    out = mm(attn_ref[...], wo_ref[...]) + mm(act_ref[...], wd_ref[...])
    store_pair(out_ref, out.astype(low), place_ref[0])


def store_pair(ref, value, place):
    near = place % 2
    ref[0, near, 0] = value[:BLK]
    ref[0, 1 - near, 0] = value[BLK:]


def by_distance(width):
    def index(i, t):
        apart = jnp.bitwise_xor(i, lax.div(t[0], 2))
        return lax.rem(apart, 2), 0, lax.div(apart, 2), 0, 0

    return pl.BlockSpec((1, 2, 1, BLK, width), index)


def merge_out(place, attn, act, w_out, w_down):
    seq, part = attn.shape
    ff = act.shape[1]
    width = w_out.shape[1]
    blk = lambda cols: pl.BlockSpec((2 * BLK, cols), lambda i, t: (i, 0))
    return pl.pallas_call(
        merge_kernel,
        grid_spec=pltpu.PrefetchScalarGridSpec(
            num_scalar_prefetch=1,
            grid=(seq // (2 * BLK),),
            in_specs=[blk(part), blk(ff), whole(w_out.shape), whole(w_down.shape)],
            out_specs=by_distance(width),
        ),
        out_shape=jax.ShapeDtypeStruct((2, 2, 2, BLK, width), low),
        compiler_params=params(),
        cost_estimate=cost(7),
        name="merge_out",
    )(place, attn, act, w_out, w_down)


def cotangent_kernel(
    c_ref, attn_ref, act_ref, slope_ref, n2_ref, wo_ref, wd_ref, _,
    ga_ref, gp_ref, pieces_ref, csum_ref, psum_ref, _out, up_scr, od_scr,
):
    i = pl.program_id(0)

    @pl.when(i == 0)
    def _():
        up_scr[...] = jnp.zeros(up_scr.shape, f32)
        od_scr[...] = jnp.zeros(od_scr.shape, f32)
        csum_ref[...] = jnp.zeros(csum_ref.shape, f32)
        psum_ref[...] = jnp.zeros(psum_ref.shape, f32)

    c = c_ref[...]
    ga_ref[...] = mm_nt(c, wo_ref[...]).astype(low)
    gp = (mm_nt(c, wd_ref[...]) * slope_ref[...]).astype(low)
    gp_ref[...] = gp
    csum_ref[...] += fold_rows(c.astype(f32), jnp.sum)
    psum_ref[...] += fold_rows(gp.astype(f32), jnp.sum)
    part = attn_ref.shape[1]
    od_scr[:part, :] += mm_tn(attn_ref[...], c)
    od_scr[part:, :] += mm_tn(act_ref[...], c)
    up_scr[...] += mm_tn(n2_ref[...], gp)

    @pl.when(i == pl.num_programs(0) - 1)
    def _():
        for o in range(16):
            rg, ch = divmod(o, 2)
            for g in range(8):
                pieces_ref[o, g * 16 : (g + 1) * 16, :] = up_scr[
                    g * 128 + rg * 16 : g * 128 + (rg + 1) * 16, ch * 256 : (ch + 1) * 256
                ]
            for b in range(4):
                pieces_ref[o, 128 + b * 32 : 160 + b * 32, :] = od_scr[
                    part + o * 32 : part + (o + 1) * 32, b * 256 : (b + 1) * 256
                ]
            for b in range(2):
                lane = ch * 512 + b * 256
                pieces_ref[o, 256 + b * 16 : 272 + b * 16, :] = od_scr[
                    rg * 16 : (rg + 1) * 16, lane : lane + 256
                ]


def cotangent_side(c_row, attn, act, slope, n2, w_out, w_down, late):
    seq, width = c_row.shape
    part = attn.shape[1]
    ff = act.shape[1]
    blk = lambda cols: pl.BlockSpec((2 * BLK, cols), lambda i: (i, 0))
    shape = jax.ShapeDtypeStruct
    return pl.pallas_call(
        cotangent_kernel,
        grid=(seq // (2 * BLK),),
        in_specs=[
            blk(width), blk(part), blk(ff), blk(ff), blk(width), whole(w_out.shape),
            whole(w_down.shape), unread,
        ],
        out_specs=[
            blk(part), blk(ff), whole((16, 288, 256)), whole((8, width)), whole((8, ff)), unread,
        ],
        out_shape=[
            shape((seq, part), low), shape((seq, ff), low), shape((16, 288, 256), f32),
            shape((8, width), f32), shape((8, ff), f32), shape(late.shape, late.dtype),
        ],
        scratch_shapes=[pltpu.VMEM((width, ff), f32), pltpu.VMEM((part + ff, width), f32)],
        input_output_aliases={7: 5},
        compiler_params=params(),
        cost_estimate=cost(14),
        name="cotangent_side",
    )(c_row, attn, act, slope, n2, w_out, w_down, late)


def backward_kernel(
    trunk_ref, q_ref, k_ref, v_ref, kt_ref, ga_ref, lse_ref, qinfo_ref, kseg_ref,
    cos_ref, sf_ref, sb_ref, *rest
):
    gqkv_ref, p_scr, dp_scr, dk_scr, dv_scr, dq_scr, d_scr = rest[-7:]
    i = pl.num_programs(0) - 1 - pl.program_id(0)

    @pl.when(pl.program_id(0) == 0)
    def _():
        dk_scr[...] = jnp.zeros(dk_scr.shape, f32)
        dv_scr[...] = jnp.zeros(dv_scr.shape, f32)

    heads = split_heads(q_ref[...])
    grads = split_heads(ga_ref[...])
    q_pair = jnp.concatenate(heads, axis=0)
    g_pair = jnp.concatenate(grads, axis=0)
    count = i * QBLK // KBLK + 1
    d_scr[...] = jnp.zeros(d_scr.shape, f32)

    def probs_of(j, masked):
        rows = pl.ds(j * KBLK, KBLK)
        keys = k_ref[rows, :]
        values = v_ref[rows, :]
        allowed = allowed_keys(kseg_ref, qinfo_ref, j, i) if masked else None
        for h in range(2):
            tile = jnp.exp2(mm_nt(keys, heads[h]) * soft_mul - lse_ref[0, h : h + 1, :])
            if masked:
                tile = jnp.where(allowed, tile, 0.0)
            back = mm_nt(values, grads[h])
            p_scr[h, j] = tile
            dp_scr[h, j] = back
            d_scr[h] += fold_rows(tile * back, jnp.sum)

    each_block(i, trunk_ref[0], count, probs_of)
    deltas = [jnp.sum(d_scr[h], axis=0, keepdims=True) for h in range(2)]
    dq_scr[...] = jnp.zeros(dq_scr.shape, f32)

    def push(j, carry):
        lows = []
        scores = []
        for h in range(2):
            probs = p_scr[h, j]
            ds = (probs * (dp_scr[h, j] - deltas[h])).astype(low)
            lows.append(probs.astype(low))
            scores.append(ds)
            part = slice(h * HD, (h + 1) * HD)
            dq_scr[part, :] += mm(kt_ref[2 * j, part, :], ds[:BLK]) + mm(
                kt_ref[2 * j + 1, part, :], ds[BLK:]
            )
        rows = pl.ds(j * KBLK, KBLK)
        dk_scr[rows, :] += mm(jnp.concatenate(scores, axis=1), q_pair)
        dv_scr[rows, :] += mm(jnp.concatenate(lows, axis=1), g_pair)
        return carry

    lax.fori_loop(0, count, push, 0)
    tables = (cos_ref[...], sf_ref[...], sb_ref[...])
    rows = pl.ds(i * QBLK, QBLK)
    part = q_ref.shape[1]
    gqkv_ref[:, :part] = turn(dq_scr[...].T * scale, *tables, -1.0).astype(low)
    gqkv_ref[:, part : 2 * part] = turn(dk_scr[rows, :] * scale, *tables, -1.0).astype(low)
    gqkv_ref[:, 2 * part :] = dv_scr[rows, :].astype(low)


def attend_backward(trunk, q, k, v, kt, grad_attn, lse, qinfo, kseg, tables, after):
    seq, part = q.shape
    steps = seq // QBLK
    last = steps - 1
    blk = lambda cols: pl.BlockSpec((QBLK, cols), lambda i, t: (last - i, 0))
    info = pl.BlockSpec((1, 8, QBLK), lambda i, t: (last - i, 0, 0))
    return pl.pallas_call(
        backward_kernel,
        grid_spec=pltpu.PrefetchScalarGridSpec(
            num_scalar_prefetch=1,
            grid=(steps,),
            in_specs=[
                blk(part), whole(k.shape), whole(v.shape), whole(kt.shape), blk(part), info, info,
                whole(kseg.shape), blk(part), blk(part), blk(part),
            ]
            + [unread] * len(after),
            out_specs=blk(3 * part),
            scratch_shapes=[
                pltpu.VMEM((2, seq // KBLK, KBLK, QBLK), f32),
                pltpu.VMEM((2, seq // KBLK, KBLK, QBLK), f32),
                pltpu.VMEM((seq, part), f32),
                pltpu.VMEM((seq, part), f32),
                pltpu.VMEM((part, QBLK), f32),
                pltpu.VMEM((2, 8, QBLK), f32),
            ],
        ),
        out_shape=jax.ShapeDtypeStruct((seq, 3 * part), low),
        compiler_params=params(),
        cost_estimate=cost(26),
        name="attend_backward",
    )(trunk, q, k, v, kt, grad_attn, lse, qinfo, kseg, *tables, *after)


def leave_kernel(
    place_ref, gqkv_ref, gp_ref, x_ref, n1_ref, cols_ref, rows_ref, csum_ref, psum_ref, *rest
):
    h_ref, keep_ref, send_ref, g_scr, v_scr, qsum_scr = rest[-6:]
    i = pl.program_id(0)
    part = gqkv_ref.shape[1]
    ff = gp_ref.shape[1]

    @pl.when(i == 0)
    def _():
        g_scr[...] = jnp.zeros(g_scr.shape, f32)
        v_scr[...] = jnp.zeros(v_scr.shape, f32)
        qsum_scr[...] = jnp.zeros(qsum_scr.shape, f32)

    gqkv = gqkv_ref[...]
    normed, _ = normalize(x_ref[...].astype(f32))
    one = mm_nt(gqkv, cols_ref[:, :part])
    two = mm_nt(gp_ref[...], cols_ref[:, part : part + ff])
    store_pair(h_ref, (one * rows_ref[0:1] + two * rows_ref[2:3]).astype(low), place_ref[0])
    v_scr[0] += fold_rows(one * normed, jnp.sum)
    v_scr[1] += fold_rows(one, jnp.sum)
    v_scr[2] += fold_rows(two * normed, jnp.sum)
    v_scr[3] += fold_rows(two, jnp.sum)
    qsum_scr[...] += fold_rows(gqkv.astype(f32), jnp.sum)
    g_scr[:, :part] += mm_tn(n1_ref[...], gqkv)

    @pl.when(i == pl.num_programs(0) - 1)
    def _():
        place = place_ref[0]
        width = csum_ref.shape[1]
        lane = lax.broadcasted_iota(jnp.int32, (1, width), 1)
        mine = (lane >= place * 128) & (lane < (place + 1) * 128)
        near = (lane >= (place % 2) * 512) & (lane < (place % 2 + 1) * 512)
        qsum = jnp.sum(qsum_scr[...], axis=0, keepdims=True)
        csum = jnp.where(mine, jnp.sum(csum_ref[...], axis=0, keepdims=True), 0.0)
        psum = jnp.sum(psum_ref[...], axis=0, keepdims=True)
        psum = jnp.where(near, jnp.concatenate([psum] * 2, axis=1), 0.0)
        rows = [jnp.sum(v_scr[n], axis=0, keepdims=True) for n in range(4)]
        for n in range(3):
            spread = jnp.concatenate([qsum[:, n * 128 : (n + 1) * 128]] * 8, axis=1)
            rows.append(jnp.where(mine, spread, 0.0))
        rows += [csum, csum]
        for n in range(4):
            rows.append(jnp.where(place // 2 == n, psum, 0.0))
        rows.append(jnp.zeros((128 - len(rows), width), f32))
        g_scr[:, part:] = jnp.concatenate(rows, axis=0).T
        for out_ref, ch in ((keep_ref, place_ref[1]), (send_ref, 1 - place_ref[1])):
            lanes = pl.ds(pl.multiple_of(ch * 256, 256), 256)
            for rg in range(8):
                for g in range(8):
                    top = g * 128 + rg * 16
                    out_ref[rg, g * 16 : (g + 1) * 16, :] = g_scr[top : top + 16, lanes]


def leave(place, gqkv, grad_pre, x_row, n1, cols, rows, csum, psum, after):
    seq, width = x_row.shape
    part3 = gqkv.shape[1]
    ff = grad_pre.shape[1]
    steps = seq // (2 * BLK)
    blk = lambda cols: pl.BlockSpec((2 * BLK, cols), lambda i, t: (i, 0))
    shape = jax.ShapeDtypeStruct
    return pl.pallas_call(
        leave_kernel,
        grid_spec=pltpu.PrefetchScalarGridSpec(
            num_scalar_prefetch=1,
            grid=(steps,),
            in_specs=[
                blk(part3), blk(ff), blk(width), blk(width), whole(cols.shape),
                whole(rows.shape), whole(csum.shape), whole(psum.shape),
            ]
            + [unread] * len(after),
            out_specs=[by_distance(width), whole((8, 128, 256)), whole((8, 128, 256))],
            scratch_shapes=[
                pltpu.VMEM((width, part3 + 128), f32),
                pltpu.VMEM((4, 8, width), f32),
                pltpu.VMEM((8, part3), f32),
            ],
        ),
        out_shape=[
            shape((2, 2, 2, BLK, width), low), shape((8, 128, 256), f32),
            shape((8, 128, 256), f32),
        ],
        compiler_params=params(),
        cost_estimate=cost(300),
        name="leave",
    )(place, gqkv, grad_pre, x_row, n1, cols, rows, csum, psum, *after)


def two_summands(tail):
    lane = lax.broadcasted_iota(jnp.int32, tail.shape, 1)
    head = tail.astype(low).astype(f32)
    rest = pltpu.roll(tail - head, 16, 1)
    return jnp.where(lane < 16, head, jnp.where(lane < 32, rest, 0.0)).astype(low)


def pair_kernel(core_ref, keep_ref, got_ref, *rest):
    out_ref = rest[-1]
    for n in range(keep_ref.shape[0]):
        total = keep_ref[n] + got_ref[n]
        out_ref[n] = total.astype(low)

        if total.shape[0] == 128:

            @pl.when(core_ref[0] == 1)
            def _(n=n, total=total):
                out_ref[n, :, 128:] = two_summands(total[:, 128:])


def sum_kernel(core_ref, got_ref, *rest):
    out_ref = rest[-1]
    total = jnp.sum(got_ref[...].astype(f32), axis=0)
    out_ref[...] = total.astype(low)

    if total.shape[0] == 128:

        @pl.when(core_ref[0] == 1)
        def _():
            tail = total[:, 128:]
            out_ref[:, 128:] = two_summands(tail + pltpu.roll(tail, 112, 1))


def pack_kernel(block_ref, *rest):
    for n in range(rest[-1].shape[0]):
        rest[-1][n] = block_ref[...]


def copies_of(block, count, after):
    return pl.pallas_call(
        pack_kernel,
        grid=(2,),
        in_specs=[whole(block.shape)] + [unread] * len(after),
        out_specs=pl.BlockSpec((count // 2,) + block.shape, lambda i: (i, 0, 0)),
        out_shape=jax.ShapeDtypeStruct((count,) + block.shape, block.dtype),
        compiler_params=params(),
        cost_estimate=cost(2),
        name="copies_of",
    )(block, *after)


def far_kernel(parts_ref, _, out_ref):
    out_ref[...] = parts_ref[0]


def far_blocks(parts, before):
    _, _, depth, local_len, width = parts.shape
    rows = local_len // 2
    return pl.pallas_call(
        far_kernel,
        grid=(2,),
        in_specs=[
            pl.BlockSpec((1, 1, depth, rows, width), lambda i: (1, 0, 0, i, 0)), unread,
        ],
        out_specs=pl.BlockSpec((1, depth, rows, width), lambda i: (0, 0, i, 0)),
        out_shape=jax.ShapeDtypeStruct((1,) + parts.shape[2:], parts.dtype),
        compiler_params=params(),
        cost_estimate=cost(2),
        name="far_blocks",
    )(parts, before)


def pair_sum(core, keep, got, after):
    count, rows, lanes = keep.shape
    block = pl.BlockSpec((count // 4, rows, lanes), lambda i, t: (i, 0, 0))
    return pl.pallas_call(
        pair_kernel,
        grid_spec=pltpu.PrefetchScalarGridSpec(
            num_scalar_prefetch=1,
            grid=(4,),
            in_specs=[block, block] + [unread] * len(after),
            out_specs=block,
        ),
        out_shape=jax.ShapeDtypeStruct(keep.shape, low),
        compiler_params=params(),
        cost_estimate=cost(4),
        name="pair_sum",
    )(core, keep, got, *after)


def sum_pieces(core, got, after):
    owners, rows, lanes = got.shape
    return pl.pallas_call(
        sum_kernel,
        grid_spec=pltpu.PrefetchScalarGridSpec(
            num_scalar_prefetch=1,
            grid=(1,),
            in_specs=[whole(got.shape)] + [unread] * len(after),
            out_specs=whole((rows, lanes)),
        ),
        out_shape=jax.ShapeDtypeStruct((rows, lanes), low),
        compiler_params=params(),
        cost_estimate=cost(2),
        name="sum_pieces",
    )(core, got, *after)


def branch_of(segment):
    return jnp.where(segment >= 5, 1 + (segment - 5) // 2, segment)


def rotary_tables(seq):
    lane = jnp.arange(128) % HD
    front = lane < ROT // 2
    back = (lane >= ROT // 2) & (lane < ROT)
    inv_freq = 10000.0 ** (-(2 * (lane % (ROT // 2))).astype(f32) / ROT)
    inv_freq = jnp.where(front | back, inv_freq, 0.0)
    angles = jnp.arange(seq).astype(f32)[:, None] * inv_freq[None, :]
    sines = jnp.sin(angles)
    return jnp.cos(angles), jnp.where(front, -sines, 0.0), jnp.where(back, sines, 0.0)


def tree_info(segment, live):
    seq = segment.shape[0]
    steps = seq // QBLK
    trunk = jnp.sum((segment == 0).astype(jnp.int32)).reshape(1)
    key_seg = jnp.broadcast_to(jnp.where(live == 1, segment, -1)[:, None], (seq, 128))
    pair = jnp.stack([segment, branch_of(segment)]).reshape(2, steps, QBLK).transpose(1, 0, 2)
    return trunk, jnp.pad(pair, ((0, 0), (0, 6), (0, 0))), key_seg


def adam_store(grad, master, first, second, rate, outs, where):
    new_master, new_first, new_second = adamw_apply(master, first, second, grad, rate)
    for ref, value in zip(outs, (new_master, new_first, new_second, new_master.astype(low))):
        ref[where] = value


def adamw_apply(master, first_mom, second_mom, gradient, learn_rate):
    first_new = adam_beta * first_mom + (1.0 - adam_beta) * gradient
    second_new = adam_beta * second_mom + (1.0 - adam_beta) * gradient * gradient
    correction = 1.0 - adam_beta**STEP
    adam_step = first_new / correction / (jnp.sqrt(second_new / correction) + adam_eps)
    master_new = master - learn_rate * (adam_step + weight_decay * master)
    return (master_new, first_new, second_new)


def adam_call(name, core, pieces, g_spec, states, block, steps, cut, rate):
    def kernel(core_ref, mine_ref, theirs_ref, m_ref, f_ref, s_ref, *outs):
        for half in range(2):
            for cols, pick in cut(pl.program_id(0), half):
                grad = jnp.where(
                    core_ref[0] == half, pick(mine_ref).astype(f32), pick(theirs_ref).astype(f32)
                )
                where = (slice(None), cols)
                adam_store(grad, m_ref[where], f_ref[where], s_ref[where], rate, outs, where)

    tab = pl.BlockSpec(block, lambda i, t: (0, i))
    shape = states[0].shape
    size = shape[0] * shape[1]
    return pl.pallas_call(
        kernel,
        grid_spec=pltpu.PrefetchScalarGridSpec(
            num_scalar_prefetch=1,
            grid=(steps,),
            in_specs=[g_spec] * 2 + [tab] * 3,
            out_specs=[tab] * 4,
        ),
        out_shape=[jax.ShapeDtypeStruct(shape, f32)] * 3 + [jax.ShapeDtypeStruct(shape, low)],
        compiler_params=params(),
        cost_estimate=cost(7),
        name=name,
    )(core, *pieces, *states)


def take(rows):
    return lambda ref: ref[:, rows, :].reshape(-1, ref.shape[2])


def update_up(core, pieces, states, rate):
    def cut(step, half):
        for s in range(2):
            lane = s * 512 + half * 256
            yield slice(lane, lane + 256), take(slice(s * 16, (s + 1) * 16))

    spec = pl.BlockSpec((8, 32, 256), lambda i, t: (0, i, 0))
    return adam_call("update_up", core, pieces, spec, states, (128, 1024), 4, cut, rate)


def update_out(core, pieces, states, rate):
    def cut(step, half):
        for b in range(2):
            lane = half * 512 + b * 256
            yield slice(lane, lane + 256), take(slice(b * 16, (b + 1) * 16))

    spec = pl.BlockSpec((8, 32, 256), lambda i, t: (0, 8, 0))
    return adam_call("update_out", core, pieces, spec, states, (128, 1024), 1, cut, rate)


def update_down(core, pieces, states, rate):
    def kernel(core_ref, mine_ref, theirs_ref, m_ref, f_ref, s_ref, *outs):
        for rg in range(8):
            for half in range(2):
                where = (slice(rg * 64 + half * 32, rg * 64 + half * 32 + 32), slice(None))
                grad = jnp.where(
                    core_ref[0] == half, mine_ref[rg].astype(f32), theirs_ref[rg].astype(f32)
                )
                adam_store(grad, m_ref[where], f_ref[where], s_ref[where], rate, outs, where)

    g_spec = pl.BlockSpec((8, 32, 256), lambda i, t: (0, 4 + i, 0))
    tab = pl.BlockSpec((512, 256), lambda i, t: (0, i))
    shape = states[0].shape
    size = shape[0] * shape[1]
    return pl.pallas_call(
        kernel,
        grid_spec=pltpu.PrefetchScalarGridSpec(
            num_scalar_prefetch=1,
            grid=(4,),
            in_specs=[g_spec] * 2 + [tab] * 3,
            out_specs=[tab] * 4,
        ),
        out_shape=[jax.ShapeDtypeStruct(shape, f32)] * 3 + [jax.ShapeDtypeStruct(shape, low)],
        compiler_params=params(),
        cost_estimate=cost(7),
        name="update_down",
    )(core, *pieces, *states)


def update_qkv(core, pieces, states, rate):
    def kernel(core_ref, mine_ref, theirs_ref, m_ref, f_ref, s_ref, *outs):
        is_mine = core_ref[0] == pl.program_id(0) // 2
        for src in range(8):
            where = (slice(None), slice(src * 128, (src + 1) * 128))
            pick = take(slice(src * 16, (src + 1) * 16))
            grad = jnp.where(is_mine, pick(mine_ref).astype(f32), pick(theirs_ref).astype(f32))
            adam_store(grad, m_ref[where], f_ref[where], s_ref[where], rate, outs, where)

    g_spec = pl.BlockSpec((8, 128, 128), lambda i, t: (0, 0, i % 2))
    tab = pl.BlockSpec((128, 1024), lambda i, t: (0, i))
    shape = states[0].shape
    size = shape[0] * shape[1]
    return pl.pallas_call(
        kernel,
        grid_spec=pltpu.PrefetchScalarGridSpec(
            num_scalar_prefetch=1,
            grid=(3,),
            in_specs=[g_spec] * 2 + [tab] * 3,
            out_specs=[tab] * 4,
        ),
        out_shape=[jax.ShapeDtypeStruct(shape, f32)] * 3 + [jax.ShapeDtypeStruct(shape, low)],
        compiler_params=params(),
        cost_estimate=cost(7),
        name="update_qkv",
    )(core, *pieces, *states)


def fold_kernel(mine_ref, one_ref, two_ref, three_ref, _, keep_ref, send_ref):
    sums = []
    for z in range(2):
        total = mine_ref[0, 0, z].astype(f32)
        for ref in (one_ref, two_ref, three_ref):
            total += ref[0, z].astype(f32)
        sums.append(total)
    keep_ref[...] = sums[0]
    send_ref[...] = sums[1].astype(low)


def fold(parts, got, before):
    _, _, _, local_len, width = parts.shape
    rows = 128
    mine = pl.BlockSpec((1, 1, 2, rows, width), lambda i: (0, 0, 0, i, 0))
    other = pl.BlockSpec((1, 2, rows, width), lambda i: (0, 0, i, 0))
    block = pl.BlockSpec((rows, width), lambda i: (i, 0))
    shape = jax.ShapeDtypeStruct((local_len, width), f32)
    return pl.pallas_call(
        fold_kernel,
        grid=(local_len // rows,),
        in_specs=[mine, other, other, other, unread],
        out_specs=[block, block],
        out_shape=[shape, jax.ShapeDtypeStruct((local_len, width), low)],
        compiler_params=params(),
        cost_estimate=cost(4),
        name="fold",
    )(parts, *got, before)


def finish_out_kernel(keep_ref, got_ref, x_ref, bias_ref, _, out_ref):
    total = keep_ref[...] + got_ref[...].astype(f32)
    out_ref[...] = (x_ref[...].astype(f32) + total + bias_ref[0:1]).astype(low)


def finish_grad_kernel(keep_ref, got_ref, x_ref, c_ref, _, out_ref):
    normed, inverse = normalize(x_ref[...].astype(f32))
    total = keep_ref[...] + got_ref[...].astype(f32)
    out_ref[...] = c_ref[...].astype(f32) + norm_back(total, normed, inverse)


def finish(kernel, name, operands, before, dtype):
    local_len, width = operands[0].shape
    rows = 128
    block = pl.BlockSpec((rows, width), lambda i: (i, 0))
    return pl.pallas_call(
        kernel,
        grid=(local_len // rows,),
        in_specs=[block if o.shape[0] == local_len else whole(o.shape) for o in operands]
        + [unread],
        out_specs=block,
        out_shape=jax.ShapeDtypeStruct((local_len, width), dtype),
        compiler_params=params(),
        cost_estimate=cost(3),
        name=name,
    )(*operands, before)


def body(
    hidden_in,
    cotangent,
    segment_ids,
    live_slots,
    w_qkv,
    w_out,
    w_up,
    w_down,
    w_vec,
    master_qkv,
    master_out,
    master_up,
    master_down,
    master_vec,
    first_qkv,
    first_out,
    first_up,
    first_down,
    first_vec,
    second_qkv,
    second_out,
    second_up,
    second_down,
    second_vec,
):
    grp = ("zl", "x")
    own = ("y", "zh", "core")
    groups = lax.axis_size(grp)
    owners = lax.axis_size(own)
    pos = lax.axis_index(grp)
    _, local_len, width = hidden_in.shape
    seq_len = local_len * groups
    rows = w_qkv.shape[0]
    ff_part = w_up.shape[1] // groups
    qkv_part = 3 * rows
    n_vec = w_vec.shape[1]
    x_local = hidden_in[0]
    c_local = cotangent[0]

    sub = rows // 8
    first = (lax.axis_index("y") * 2 + lax.axis_index("core")) * sub

    def cut(table):
        return lax.dynamic_slice_in_dim(table, first, sub, 0)

    send_w = jnp.concatenate(
        [
            cut(w_qkv).reshape(sub, 3, groups, rows).transpose(2, 0, 1, 3).reshape(groups, sub, qkv_part),
            cut(w_up).reshape(sub, groups, ff_part).transpose(1, 0, 2),
            jnp.broadcast_to(jnp.pad(cut(w_vec), ((0, 0), (0, 128 - n_vec)))[None], (groups, sub, 128)),
        ],
        axis=2,
    )
    part_w = lax.all_to_all(send_w, grp, 0, 0)
    wide = lax.all_to_all(jnp.broadcast_to(part_w[None], (8,) + part_w.shape), ("y", "core"), 0, 0)
    vec_cols = wide[:, :, :, qkv_part + ff_part : qkv_part + ff_part + n_vec]
    vectors = vec_cols.astype(f32).transpose(3, 1, 0, 2).reshape(n_vec, width)
    x_row = lax.all_gather(x_local, grp, axis=0, tiled=True)
    c_row = lax.all_gather(c_local, grp, axis=0, tiled=True)

    gain_rows = jnp.pad(vectors[:4], ((0, 4), (0, 0)))
    bias_qkv = w_vec[:, 4:7].astype(f32).T.reshape(1, qkv_part)
    bias_up = lax.dynamic_slice_in_dim(vectors[9:].reshape(-1), pos * ff_part, ff_part)[None]
    core = lax.axis_index("core").astype(jnp.int32).reshape(1)
    place = jnp.concatenate([pos.astype(jnp.int32).reshape(1), core])
    tables = rotary_tables(seq_len)
    trunk, qinfo, kseg = tree_info(segment_ids[0], live_slots[0])

    q, k, v, kt, vt, n1, n2, act, slope, cols = enter(
        x_row, wide, gain_rows, bias_qkv, bias_up, tables, (kseg, qinfo)
    )
    attn, lse = attend_forward(trunk, q, k, vt, qinfo, kseg)
    out_part = merge_out(place, attn, act, w_out, w_down)
    grad_attn, grad_pre, pieces_a, csum, psum, out_late = cotangent_side(
        c_row, attn, act, slope, n2, w_out, w_down, out_part
    )

    def along_x(block, d):
        return lax.ppermute(block, "x", [(g, g ^ d) for g in range(4)])

    def hand_out(parts, before):
        return [
            along_x(parts[0, 1:2], 1),
            along_x(parts[1, 0:1] if before is None else far_blocks(parts, before), 2),
            along_x(parts[1, 1:2], 3),
        ]

    def add_up(parts, got, before):
        keep, send = fold(parts, got, before)
        return keep, lax.ppermute(send, "zl", [(0, 1), (1, 0)])

    def across(block):
        return lax.ppermute(block, "core", [(0, 1), (1, 0)])

    def turn_over(pieces):
        return lax.all_to_all(pieces, ("y", "zh"), 0, 0)

    def spread(block, after):
        mine = turn_over(copies_of(block, owners // 2, after))
        return mine, across(mine)

    gqkv = attend_backward(trunk, q, k, v, kt, grad_attn, lse, qinfo, kseg, tables, ())
    sum_a = lax.psum_scatter(
        pieces_a.reshape(owners * 288, 256), own, scatter_dimension=0, tiled=True
    ).astype(low)
    got_out = hand_out(out_late, gqkv)
    h_part, keep_b, send_b = leave(
        place, gqkv, grad_pre, x_row, n1, cols, gain_rows, csum, psum, (got_out[0], got_out[2])
    )
    got_h = hand_out(h_part, None)
    got_b = turn_over(pair_sum(core, keep_b, across(send_b), (got_out[1],)))
    sum_b = sum_pieces(core, got_b, ())
    both = jnp.stack([sum_a[:128].reshape(groups, 16, 256), sum_b.reshape(groups, 16, 256)], axis=1)
    turned = lax.all_to_all(both, grp, 0, 0)
    all_a = spread(jnp.concatenate([turned[:, 0].reshape(128, 256), sum_a[128:]], axis=0), got_h[::2])
    all_b = spread(turned[:, 1].reshape(128, 256), (all_a[0], got_h[1]))
    halves = [part[:, :, 128:160].astype(f32) for part in all_b]
    vec_sums = jnp.where(core[0] == 1, halves[0], halves[1]).reshape(8, groups, 16, 32)
    vec_grad = jnp.sum(vec_sums[..., :16] + vec_sums[..., 16:], axis=1).reshape(rows, 16)[:, :n_vec]

    bias_rows = jnp.broadcast_to((vectors[7] + vectors[8])[None], (8, width))
    results = [
        update_qkv(core, all_b, (master_qkv, first_qkv, second_qkv), learn_rates[0]),
        update_out(core, all_a, (master_out, first_out, second_out), learn_rates[1]),
        update_up(core, all_a, (master_up, first_up, second_up), learn_rates[2]),
        update_down(core, all_a, (master_down, first_down, second_down), learn_rates[3]),
    ]
    layer_out = finish(
        finish_out_kernel,
        "finish_out",
        (*add_up(out_late, got_out, all_a[0]), x_local, bias_rows),
        results[1][3],
        low,
    )
    input_grad = finish(
        finish_grad_kernel,
        "finish_grad",
        (*add_up(h_part, got_h, all_b[0]), x_local, c_local),
        results[2][3],
        f32,
    )
    vec_new = adamw_apply(master_vec, first_vec, second_vec, vec_grad, learn_rates[4])
    results.append(vec_new + (vec_new[0].astype(low),))
    return (
        (layer_out[None], input_grad[None])
        + tuple(r[0] for r in results)
        + tuple(r[1] for r in results)
        + tuple(r[2] for r in results)
        + tuple(r[3] for r in results)
    )


def solution(mesh):
    fine = jax.sharding.Mesh(
        mesh.devices.reshape(2, 4, 4, 2, 2), ("zl", "x", "y", "zh", "core")
    )
    grp = ("zl", "x")
    own = ("y", "zh", "core")
    act_spec = P(own, grp, None)
    id_spec = P(own, None)
    tab_spec = P(grp, None)
    return jax.shard_map(
        body,
        mesh=fine,
        in_specs=(act_spec,) * 2 + (id_spec,) * 2 + (tab_spec,) * 20,
        out_specs=(act_spec,) * 2 + (tab_spec,) * 20,
        check_vma=False,
    )
```
